32 devices in a mesh: ctx: 4 (over z), head: 4 (over x, core), row: 2 (over y).
Axes of the slice: x: 2, y: 2, z: 4, core: 2. Of those that a mesh axis runs over, the one named last changes fastest.
Arguments:
- hidden: bfloat16 [384, 8192], P(('ctx', 'row')), may hold values from -6 to 6
- norm_gain: bfloat16 [8192], replicated, may hold values from 0.099609375 to 1.8984375
- q_weight: bfloat16 [8192, 4096], P(None, ('head', 'row')), may hold values from -0.09375 to 0.09375
- q_bias: bfloat16 [4096], P(('head', 'row')), may hold values from -3 to 3
- key_weight: bfloat16 [8192, 512], P(None, 'head'), may hold values from -0.0625 to 0.0625
- key_bias: bfloat16 [512], P('head'), may hold values from -3 to 3
- value_weight: bfloat16 [8192, 512], P(None, 'head'), may hold values from -0.0625 to 0.0625
- value_bias: bfloat16 [512], P('head'), may hold values from -3 to 3
- o_weight: bfloat16 [4096, 8192], P(('head', 'row')), may hold values from -4 to 4
- cached_key_rows: bfloat16 [16384, 512], P('ctx', 'head'), may hold values from -256 to 256
- cached_value_rows: bfloat16 [16384, 512], P('ctx', 'head'), may hold values from -6 to 6
- keep_blocks: int32 [4, 8], P('ctx'), may hold values from 0 to 31, as said below
- kept_counts: int32 [4], replicated, may hold values from 2 to 8, as said below
- span_start: int32 [1], replicated, may hold values from 16384 to 20479
Outputs:
- output: bfloat16 [384, 8192], P('ctx', ('head', 'row'))
The draws below stay inside these ranges and needn't reach their ends.
Inputs may be any that keep to these rules, and one draw needn't show every extreme that they name: `keep_blocks`: row g lists in increasing order the kept_counts[g] distinct kept blocks among group g's 32 prefix blocks; its remaining entries are 0. `kept_counts`: one group keeps 8 blocks and another keeps 8 // 4.
All inputs are finite; a program needn't handle non-finite values.
Results may differ from the reference program's by a relative error of at most 0.014.
Values may be sent and summed in bfloat16 or wider, within the bound.
No kernel may reach another device: no remote copies, remote signals or barrier semaphores. Data moves between devices by JAX's collectives and lax.ppermute only.
A program may use at most 128 MiB of HBM per device.

```python
import jax
import jax.numpy as jnp
from jax import lax

MODEL_WIDTH = 8192
HEAD_WIDTH = 128
QUERY_HEADS = 32
KEY_VALUE_HEADS = 4
BLOCK = 128
PB_G = 32
KEEP = 8
SPAN_TOKENS = 384
PREFIX_LENGTH = 16384
N_CTX = 4


def keep_plan(key):
    key_count, key_top, key_low, key_order = jax.random.split(key, 4)
    counts = jax.random.randint(key_count, (N_CTX,), KEEP // 4, KEEP // 2 + 1)
    busiest = jax.random.randint(key_top, (), 0, N_CTX)
    lightest = (busiest + jax.random.randint(key_low, (), 1, N_CTX)) % N_CTX
    counts = counts.at[busiest].set(KEEP).at[lightest].set(KEEP // 4)
    orders = jax.vmap(lambda sub_key: jax.random.permutation(sub_key, PB_G))(jax.random.split(key_order, N_CTX))
    chosen = orders[:, :KEEP]
    slot_index = jnp.arange(KEEP, dtype=jnp.int32)
    marked = jnp.where(slot_index[None, :] < counts[:, None], chosen, PB_G)
    ordered = jnp.sort(marked, axis=1)
    blocks = jnp.where(ordered < PB_G, ordered, 0)
    return (blocks.astype(jnp.int32), counts.astype(jnp.int32))


def draw_keep_blocks(key, part):
    return keep_plan(key)[0]


def draw_kept_counts(key, part):
    return keep_plan(key)[1]


def draw_cached_key_rows(key, part):
    key = jax.random.fold_in(key, 7)
    key_rotary_base = jax.random.fold_in(key, 0)
    rotary_base = jax.random.normal(key_rotary_base, (PREFIX_LENGTH, KEY_VALUE_HEADS * HEAD_WIDTH), jnp.float32)
    return jnp.clip(rotary_base, -256.0, 256.0).astype(jnp.bfloat16)


def with_spikes(result, stream_key, source, target, shards_of, factor):
    owner, partner = [(jnp.arange(result.shape[dim]) // (result.shape[dim] // shards_of)).reshape([-1 if axis == dim else 1 for axis in range(result.ndim)]) for dim in (source, target)]
    chosen = jax.random.permutation(stream_key, shards_of)[partner]
    strong = (owner == chosen) | (owner == (partner + shards_of // 2) % shards_of)
    return jnp.where(strong, factor * result, result)


def level_of(stream_key, dims, cuts, smallest, largest):
    def one(position, shards_of):
        steps = jax.random.uniform(jax.random.fold_in(jax.random.fold_in(stream_key, 6), position), (shards_of,), jnp.float32, smallest / len(cuts), largest / len(cuts))
        return jnp.repeat(jnp.exp(steps), dims[position] // shards_of).reshape((-1,) + (1,) * (len(dims) - position - 1))

    level = one(*cuts[0])
    for cut in cuts[1:]:
        level = level * one(*cut)
    return level


def centred(rng, extent, deviation, reach, cuts=(), held_as=jnp.bfloat16):
    drawn = jax.random.normal(rng, extent, jnp.float32) * deviation
    if len(cuts) > 0:
        drawn = level_of(rng, extent, cuts, -0.22, 0.18) * drawn
    return jnp.clip(drawn, min=-reach, max=reach).astype(held_as)


def heavy_noise(stream_key, extent, scale, most, cuts, heavy, kind=jnp.bfloat16):
    array = scale * jax.random.normal(stream_key, extent, jnp.float32)
    if cuts:
        array = array * level_of(stream_key, extent, cuts, -0.22, 0.18)
    return jnp.clip(with_spikes(array, jax.random.fold_in(stream_key, 3), *heavy), -most, most).astype(kind)


def setup_inputs(seed: int = 0) -> dict:
    key_list = jax.random.split(jax.random.key(seed), 15)
    hidden = centred(key_list[0], (SPAN_TOKENS, MODEL_WIDTH), 1.0, 6.0, ((0, 8),))
    norm_gain = jnp.clip(1.0 + 0.18 * jax.random.normal(key_list[1], (MODEL_WIDTH,), jnp.float32), 0.099609375, 1.8984375).astype(jnp.bfloat16)
    q_weight = centred(key_list[2], (MODEL_WIDTH, QUERY_HEADS * HEAD_WIDTH), (MODEL_WIDTH // 2) ** -0.5, 0.09375, ((1, 8),))
    q_bias = centred(key_list[3], (QUERY_HEADS * HEAD_WIDTH,), 0.5, 3.0, ((0, 8),))
    key_weight = centred(key_list[4], (MODEL_WIDTH, KEY_VALUE_HEADS * HEAD_WIDTH), MODEL_WIDTH ** -0.5, 0.0625, ((1, 4),))
    key_bias = centred(key_list[5], (KEY_VALUE_HEADS * HEAD_WIDTH,), 0.5, 3.0, ((0, 4),))
    value_weight = centred(key_list[6], (MODEL_WIDTH, KEY_VALUE_HEADS * HEAD_WIDTH), MODEL_WIDTH ** -0.5, 0.0625, ((1, 4),))
    value_bias = centred(key_list[7], (KEY_VALUE_HEADS * HEAD_WIDTH,), 0.5, 3.0, ((0, 4),))
    o_weight = heavy_noise(key_list[8], (QUERY_HEADS * HEAD_WIDTH, MODEL_WIDTH), (max(1, QUERY_HEADS * HEAD_WIDTH // 1024)) ** -0.5, 4.0, ((0, 8),), (0, 1, 8, 2.0))
    cached_key_rows = draw_cached_key_rows(jax.random.fold_in(key_list[14], 71), 0)
    cached_value_rows = centred(key_list[10], (PREFIX_LENGTH, KEY_VALUE_HEADS * HEAD_WIDTH), 1.0, 6.0, ((0, 4), (1, 4)))
    keep_blocks = draw_keep_blocks(jax.random.fold_in(key_list[14], 71), 0)
    kept_counts = draw_kept_counts(jax.random.fold_in(key_list[14], 71), 0)
    span_start = jax.random.randint(key_list[13], (1,), PREFIX_LENGTH, PREFIX_LENGTH + 4096).astype(jnp.int32)
    return {"hidden": hidden, "norm_gain": norm_gain, "q_weight": q_weight, "q_bias": q_bias, "key_weight": key_weight, "key_bias": key_bias, "value_weight": value_weight, "value_bias": value_bias, "o_weight": o_weight, "cached_key_rows": cached_key_rows, "cached_value_rows": cached_value_rows, "keep_blocks": keep_blocks, "kept_counts": kept_counts, "span_start": span_start}


def apply_rotary(values, token_positions):
    middle = values.shape[-1] // 2
    steps_range = jnp.arange(middle, dtype=jnp.float32)
    frequency = 1000000.0 ** (-2.0 * steps_range / values.shape[-1])
    angles = token_positions.astype(jnp.float32)[:, None] * frequency[None, :]
    cosine = jnp.cos(angles)[:, None, :]
    sine_part = jnp.sin(angles)[:, None, :]
    first_half = values[..., :middle]
    second_half = values[..., middle:]
    return jnp.concatenate([first_half * cosine - second_half * sine_part, second_half * cosine + first_half * sine_part], axis=-1)

def reference(hidden, norm_gain, q_weight, q_bias, key_weight, key_bias, value_weight, value_bias, o_weight, cached_key_rows, cached_value_rows, keep_blocks, kept_counts, span_start):
    widened = hidden.astype(jnp.float32)
    rms_factor = lax.rsqrt(lax.optimization_barrier(jnp.mean(widened * widened, axis=-1, keepdims=True)) + 1e-06)
    normed = (widened * rms_factor * norm_gain.astype(jnp.float32)).astype(jnp.bfloat16)
    token_positions = span_start[0] + jnp.arange(SPAN_TOKENS, dtype=jnp.int32)
    queries = jnp.dot(normed, q_weight, preferred_element_type=jnp.float32) + q_bias.astype(jnp.float32)
    queries = apply_rotary(queries.reshape(SPAN_TOKENS, QUERY_HEADS, HEAD_WIDTH), token_positions).astype(jnp.bfloat16)
    fresh_keys = jnp.dot(normed, key_weight, preferred_element_type=jnp.float32) + key_bias.astype(jnp.float32)
    fresh_keys = apply_rotary(fresh_keys.reshape(SPAN_TOKENS, KEY_VALUE_HEADS, HEAD_WIDTH), token_positions).astype(jnp.bfloat16)
    fresh_values = (jnp.dot(normed, value_weight, preferred_element_type=jnp.float32) + value_bias.astype(jnp.float32)).astype(jnp.bfloat16)
    fresh_values = fresh_values.reshape(SPAN_TOKENS, KEY_VALUE_HEADS, HEAD_WIDTH)
    slot_index = jnp.arange(KEEP, dtype=jnp.int32)
    block_ids = jnp.arange(N_CTX, dtype=jnp.int32)[:, None] * PB_G + keep_blocks.astype(jnp.int32)
    row_numbers = (block_ids[:, :, None] * BLOCK + jnp.arange(BLOCK, dtype=jnp.int32)[None, None, :]).reshape(-1)
    live_slots = jnp.broadcast_to((slot_index[None, :] < kept_counts[:, None])[:, :, None], (N_CTX, KEEP, BLOCK)).reshape(-1)
    retained_keys = jnp.take(cached_key_rows, row_numbers, axis=0).reshape(-1, KEY_VALUE_HEADS, HEAD_WIDTH)
    retained_values = jnp.take(cached_value_rows, row_numbers, axis=0).reshape(-1, KEY_VALUE_HEADS, HEAD_WIDTH)
    causal_mask = jnp.arange(SPAN_TOKENS)[:, None] >= jnp.arange(SPAN_TOKENS)[None, :]
    query_group_width = QUERY_HEADS // KEY_VALUE_HEADS
    score_scale = 1.0 / HEAD_WIDTH ** 0.5

    def one_head(head_index):
        kv_head = head_index // query_group_width
        query_rows = lax.dynamic_index_in_dim(queries, head_index, 1, keepdims=False)
        prefix_keys = lax.dynamic_index_in_dim(retained_keys, kv_head, 1, keepdims=False)
        prefix_values = lax.dynamic_index_in_dim(retained_values, kv_head, 1, keepdims=False)
        span_keys = lax.dynamic_index_in_dim(fresh_keys, kv_head, 1, keepdims=False)
        span_values = lax.dynamic_index_in_dim(fresh_values, kv_head, 1, keepdims=False)
        prefix_scores = jnp.dot(query_rows, prefix_keys.T, preferred_element_type=jnp.float32) * score_scale
        span_scores = jnp.dot(query_rows, span_keys.T, preferred_element_type=jnp.float32) * score_scale
        prefix_scores = jnp.where(live_slots[None, :], prefix_scores, -jnp.inf)
        span_scores = jnp.where(causal_mask, span_scores, -jnp.inf)
        row_top = jnp.maximum(prefix_scores.max(axis=-1), span_scores.max(axis=-1))[:, None]
        prefix_exp = jnp.exp(prefix_scores - row_top)
        span_exp = jnp.exp(span_scores - row_top)
        denominator = prefix_exp.sum(axis=-1) + span_exp.sum(axis=-1)
        blended = jnp.dot(prefix_exp.astype(jnp.bfloat16), prefix_values, preferred_element_type=jnp.float32)
        blended = blended + jnp.dot(span_exp.astype(jnp.bfloat16), span_values, preferred_element_type=jnp.float32)
        return (blended / denominator[:, None]).astype(jnp.bfloat16)
    heads_out = lax.map(one_head, jnp.arange(QUERY_HEADS, dtype=jnp.int32))
    attended = jnp.transpose(heads_out, (1, 0, 2)).reshape(SPAN_TOKENS, QUERY_HEADS * HEAD_WIDTH)
    return jnp.dot(attended, o_weight, preferred_element_type=jnp.float32).astype(jnp.bfloat16)
```

```python
import functools
import math

import jax
import jax.numpy as jnp
from jax import lax
from jax.experimental import pallas as pl
from jax.experimental.pallas import tpu as pltpu
from jax.sharding import PartitionSpec as P

BLOCK = 128
CORES = 2
COLUMN_PIECES = 8
NORM_ROWS = 16
F32 = jnp.float32
BF16 = jnp.bfloat16
ANYWHERE = pl.BlockSpec(memory_space=pl.ANY)
IN_VMEM = pl.BlockSpec(memory_space=pltpu.VMEM)
IN_SMEM = pl.BlockSpec(memory_space=pltpu.SMEM)
IN_HBM = pl.BlockSpec(memory_space=pltpu.HBM)
VMEM_BYTES = 6 * 1024 * 1024


def params(needed=0):
    return pltpu.CompilerParams(vmem_limit_bytes=VMEM_BYTES + int(needed))


def in_hbm(value):
    return pltpu.with_memory_space_constraint(value, pltpu.HBM)


def in_vmem(value):
    return pltpu.with_memory_space_constraint(value, pltpu.VMEM)


def cost(weight):
    return pl.CostEstimate(flops=weight * 10**8, bytes_accessed=10**4, transcendentals=0)


def run_copies(pairs, sems):
    copies = [
        pltpu.make_async_copy(source, target, sems.at[index])
        for index, (source, target) in enumerate(pairs)
    ]
    for copy in copies:
        copy.start()
    return copies


def column_copies(width, which, weight_ref, out_ref, sems):
    pieces, parts = sems.shape
    depth = out_ref.shape[0] // pieces
    copies = []
    for piece in range(pieces):
        rows = pl.ds(piece * depth, depth)
        pairs = []
        for part in range(parts):
            start = pl.multiple_of((part * CORES + which) * width, width)
            target = out_ref.at[rows, pl.ds(part * width, width)]
            pairs.append((weight_ref.at[rows, pl.ds(start, width)], target))
        copies += run_copies(pairs, sems.at[piece])
    return copies


def piece_row(piece):
    rows = lax.axis_size("row")
    return lax.rem(lax.axis_index("row") + rows - piece, rows)


def first_kernel(
    keep_ref,
    hidden_ref,
    gain_ref,
    keys_ref,
    values_ref,
    normed_ref,
    half_ref,
    prefix_ref,
    raw,
    kept,
    gains,
    row_sems,
    block_sems,
    small_sems,
):
    rows, width = raw.shape
    half = width // CORES
    core = lax.rem(lax.axis_index("head"), CORES)
    slots = keep_ref.shape[1]
    list_copy, gain_copy = run_copies([(keep_ref, kept), (gain_ref, gains)], small_sems)
    steps = [pl.ds(first, NORM_ROWS) for first in range(0, rows, NORM_ROWS)]
    arriving = run_copies([(hidden_ref.at[at, :], raw.at[at, :]) for at in steps], row_sems)
    list_copy.wait()
    pairs = []
    for slot in range(slots):
        block = pl.ds(pl.multiple_of(kept[0, slot] * BLOCK, BLOCK), BLOCK)
        for kind, source in enumerate((keys_ref, values_ref)):
            pairs.append((source.at[block, :], prefix_ref.at[kind, pl.ds(slot * BLOCK, BLOCK), :]))
    others = run_copies(pairs, block_sems)
    gain_copy.wait()
    gain = gains[...].astype(F32)
    lanes = gain.shape[1]
    for copy in arriving:
        copy.wait()
    for at in steps:
        wide = raw[at, :].astype(F32)
        squares = jnp.sum(wide * wide, axis=1, keepdims=True)
        factor = lax.rsqrt(squares * (1.0 / width) + 1e-06)
        for place in range(width // lanes):
            columns = slice(place * lanes, (place + 1) * lanes)
            scaled = wide[:, columns] * factor * gain[place : place + 1, :]
            normed_ref[at, columns] = scaled.astype(BF16)
        half_ref[at, :] = normed_ref[at, pl.ds(pl.multiple_of(core * half, half), half)]
    for copy in others:
        copy.wait()


def first(keep_blocks, hidden, gain, keys, values):
    rows, width = hidden.shape
    slots = keep_blocks.shape[1]
    prefix_shape = (2, slots * BLOCK, keys.shape[1])
    return pl.pallas_call(
        first_kernel,
        out_shape=(
            jax.ShapeDtypeStruct((rows, width), BF16),
            jax.ShapeDtypeStruct((rows, width // CORES), BF16),
            pltpu.VMEM(prefix_shape, BF16),
        ),
        in_specs=[IN_HBM] * 5,
        out_specs=(IN_VMEM,) * 3,
        scratch_shapes=[
            pltpu.VMEM((rows, width), BF16),
            pltpu.SMEM((1, slots), jnp.int32),
            pltpu.VMEM(gain.shape, BF16),
            pltpu.SemaphoreType.DMA((rows // NORM_ROWS,)),
            pltpu.SemaphoreType.DMA((2 * slots,)),
            pltpu.SemaphoreType.DMA((2,)),
        ],
        compiler_params=params(8 * rows * width + 2 * math.prod(prefix_shape)),
        cost_estimate=cost(0),
        name="first",
    )(*(in_hbm(value) for value in (keep_blocks, hidden, gain, keys, values)))


def rotated(values, cosine, sine):
    return (values * cosine + pltpu.roll(values, values.shape[1] // 2, 1) * sine).astype(BF16)


def finish(total, pieces, rows, bias_ref, turn_ref, out_ref, span_ref=None):
    heads, size = bias_ref.shape[0] - 2, bias_ref.shape[1]
    for place, piece in enumerate(pieces):
        turns = pl.ds(pl.multiple_of(piece_row(piece) * rows, 16), rows)
        cosine, sine = turn_ref[0, turns, :], turn_ref[1, turns, :]
        part = total[place * rows : (place + 1) * rows]

        def columns(head):
            return part[:, head * size : (head + 1) * size] + bias_ref[head : head + 1, :]

        for head in range(heads):
            at = (place * heads + head) * rows
            out_ref[at : at + rows, :] = rotated(columns(head), cosine, sine)
        if span_ref is not None:
            span_ref[0] = rotated(columns(heads), cosine, sine)
            span_ref[1] = columns(heads + 1).astype(BF16)


def project_own_kernel(
    chunks,
    normed,
    q_weight,
    key_weight,
    value_weight,
    q_bias,
    key_bias,
    value_bias,
    turn_ref,
    out_ref,
    span_ref,
    weights,
    bias_ref,
    q_raw,
    key_raw,
    value_raw,
    bias_sems,
    sems,
):
    own_rows, width = normed.shape
    depth = width // chunks
    raw = (q_raw, key_raw, value_raw)
    few = run_copies(list(zip((q_bias, key_bias, value_bias), raw, strict=True)), bias_sems)
    copies = []
    for chunk in range(chunks):
        rows = pl.ds(chunk * depth, depth)
        at = 0
        pairs = []
        for source in (q_weight, key_weight, value_weight):
            size = source.shape[1]
            pairs.append((source.at[rows, :], weights.at[rows, pl.ds(at, size)]))
            at += size
        copies.append(run_copies(pairs, sems.at[chunk]))
    total = jnp.zeros((own_rows, weights.shape[1]), F32)
    for chunk in range(chunks):
        for copy in copies[chunk]:
            copy.wait()
        span = slice(chunk * depth, (chunk + 1) * depth)
        total = total + jnp.dot(normed[:, span], weights[span, :], preferred_element_type=F32)
    at = 0
    for copy, bias in zip(few, raw, strict=True):
        copy.wait()
        bias_ref[at : at + bias.shape[0], :] = bias[...].astype(F32)
        at += bias.shape[0]
    finish(total, [0], own_rows, bias_ref, turn_ref, out_ref, span_ref)


def project_own(normed, weights, biases, turns):
    own_rows, width = normed.shape
    heads, head_size = biases[0].shape
    columns = (heads + 2) * head_size
    chunks = 8
    return pl.pallas_call(
        functools.partial(project_own_kernel, chunks),
        out_shape=(
            jax.ShapeDtypeStruct((heads * own_rows, head_size), BF16),
            jax.ShapeDtypeStruct((2, own_rows, head_size), BF16),
            pltpu.VMEM((width, columns), BF16),
            jax.ShapeDtypeStruct((heads + 2, head_size), F32),
        ),
        in_specs=[IN_VMEM] + [IN_HBM] * 6 + [IN_VMEM],
        out_specs=(IN_VMEM,) * 4,
        scratch_shapes=[
            *(pltpu.VMEM(bias.shape, BF16) for bias in biases),
            pltpu.SemaphoreType.DMA((3,)),
            pltpu.SemaphoreType.DMA((chunks, 3)),
        ],
        compiler_params=params(2 * width * columns),
        cost_estimate=cost(200),
        name="project_own",
    )(normed, *(in_hbm(value) for value in (*weights, *biases)), turns)


def half_rows(weights, mine, columns):
    half = weights.shape[0] // CORES
    core = lax.rem(lax.axis_index("head"), CORES)
    first = pl.multiple_of((core if mine else 1 - core) * half, half)
    return weights[pl.ds(first, half), :columns]


def project_near_kernel(near_ref, weights, out_ref):
    out_ref[...] = jnp.dot(
        near_ref[...], half_rows(weights, True, out_ref.shape[1]), preferred_element_type=F32
    )


def project_near(near, weights, columns):
    rows = near.shape[0]
    return pl.pallas_call(
        project_near_kernel,
        out_shape=jax.ShapeDtypeStruct((rows, columns), F32),
        in_specs=[IN_VMEM] * 2,
        out_specs=IN_VMEM,
        compiler_params=params(12 * rows * columns),
        cost_estimate=cost(50),
        name="project_near",
    )(near, in_vmem(weights))


def project_far_kernel(own_rows, far_ref, weights, part_ref, bias_ref, turn_ref, out_ref):
    total = part_ref[...] + jnp.dot(
        far_ref[...], half_rows(weights, False, part_ref.shape[1]), preferred_element_type=F32
    )
    pieces = range(1, far_ref.shape[0] // own_rows + 1)
    finish(total, pieces, own_rows, bias_ref, turn_ref, out_ref)


def project_far(own_rows, far, weights, part, biases, turns):
    rows, columns = part.shape
    head_size = biases.shape[1]
    return pl.pallas_call(
        functools.partial(project_far_kernel, own_rows),
        out_shape=jax.ShapeDtypeStruct((columns // head_size * rows, head_size), BF16),
        in_specs=[IN_VMEM] * 5,
        out_specs=IN_VMEM,
        compiler_params=params(12 * rows * columns),
        cost_estimate=cost(0),
        name="project_far",
    )(far, in_vmem(weights), part, biases, turns)


def pack_rows_kernel(own_ref, near_ref, out_ref):
    out_ref[0] = own_ref[...]
    out_ref[1] = near_ref[...]


def pack_rows(own, near):
    return pl.pallas_call(
        pack_rows_kernel,
        out_shape=jax.ShapeDtypeStruct((2, *own.shape), BF16),
        in_specs=[IN_VMEM] * 2,
        out_specs=IN_VMEM,
        compiler_params=params(),
        cost_estimate=cost(0),
        name="pack_rows",
    )(own, near)


def quotient(values, divisor, most):
    shift = 20
    factor = -(-(1 << shift) // divisor)
    assert all((i * factor) >> shift == i // divisor for i in range(most))
    assert most * factor < 1 << 31
    return lax.shift_right_logical(values * factor, shift)


def token_ids(shape, axis, own_rows, repeats):
    count = shape[axis]
    place = lax.broadcasted_iota(jnp.int32, shape, axis)
    length = own_rows * repeats
    start = jnp.full(shape, piece_row(0) * own_rows, jnp.int32)
    for piece in range(1, count // length):
        start = jnp.where(place >= piece * length, piece_row(piece) * own_rows, start)
    return place - own_rows * quotient(place, own_rows, count) + start


def products(queries, keys):
    return lax.dot_general(queries, keys, (((1,), (1,)), ((), ())), preferred_element_type=F32)


def settle(base, scores, values, top, state=None):
    total = jnp.zeros(top.shape, F32)
    blend = jnp.zeros((top.shape[0], values[0].shape[1]), F32)
    if state is not None:
        shrink = jnp.exp2((state[0] - top) * base)
        total = state[1] * shrink
        blend = state[2] * shrink
    for part, value in zip(scores, values, strict=True):
        weights = jnp.exp2((part - top) * base)
        total = total + jnp.sum(weights, axis=1, keepdims=True)
        blend = blend + jnp.dot(weights.astype(BF16), value, preferred_element_type=F32)
    return top, total, blend


def largest(scores):
    top = None
    for part in scores:
        peak = jnp.max(part, axis=1, keepdims=True)
        top = peak if top is None else jnp.maximum(top, peak)
    return top


def neighbour_group():
    group = lax.axis_index("ctx")
    return group + 1 - 2 * lax.rem(group, 2)


def by_counts(counts_ref, slots, body):
    group, near = lax.axis_index("ctx"), neighbour_group()
    few = slots // 2
    for own_slots in (few, slots):
        for near_slots in (few, slots):
            own_fits = (counts_ref[group] <= few) == (own_slots == few)
            near_fits = (counts_ref[near] <= few) == (near_slots == few)
            pl.when(jnp.logical_and(own_fits, near_fits))(
                functools.partial(body, (own_slots, near_slots))
            )


def prefix_part(queries, counts_ref, prefix_refs, slots):
    scores, values = [], []
    places = (lax.axis_index("ctx"), neighbour_group())
    for group, ref, many in zip(places, prefix_refs, slots, strict=True):
        rows = slice(0, many * BLOCK)
        live = lax.broadcasted_iota(jnp.int32, (1, many * BLOCK), 1) < counts_ref[group] * BLOCK
        scores.append(jnp.where(live, products(queries, ref[0, rows, :]), -jnp.inf))
        values.append(ref[1, rows, :])
    return scores, values


def columns_of(values, rows):
    lane = lax.broadcasted_iota(jnp.int32, (rows, BLOCK), 1)
    tile = jnp.zeros((rows, BLOCK), F32)
    for place, value in enumerate(values):
        tile = jnp.where(lane == place, value, tile)
    return tile


def three_parts(values):
    high = values.astype(BF16).astype(F32)
    middle = (values - high).astype(BF16).astype(F32)
    return [high, middle, (values - high - middle).astype(BF16).astype(F32)]


def tail_rows(count):
    tiles = -(-count // BLOCK)
    return tiles, -(-8 * tiles // 16) * 16


def pack_state(out_ref, top, total, blend):
    count = top.shape[0]
    out_ref[:count, :] = blend.astype(BF16)
    tiles, tail = tail_rows(count)
    tile = columns_of(three_parts(top) + three_parts(total), count)
    if tiles * BLOCK > count:
        tile = jnp.concatenate([tile, jnp.zeros((tiles * BLOCK - count, BLOCK), F32)], axis=0)
    lines = jnp.transpose(tile)[:8]
    rows = [lines[:, i * BLOCK : (i + 1) * BLOCK] for i in range(tiles)]
    if tail > 8 * tiles:
        rows.append(jnp.zeros((tail - 8 * tiles, BLOCK), F32))
    out_ref[count:, :] = jnp.concatenate(rows, axis=0).astype(BF16)


def span_part(span_refs, near, which):
    return jnp.concatenate([ref[near, which] for ref in span_refs], axis=0)


def visit_kernel(base, by, counts_ref, batch_ref, own_prefix, near_prefix, *refs):
    span_refs, out_ref = refs[:-1], refs[-1]
    groups = lax.axis_size("ctx")
    group = lax.axis_index("ctx")
    source = lax.rem(group + groups - by, groups)

    def body(slots):
        queries = batch_ref[...]
        scores, values = prefix_part(queries, counts_ref, (own_prefix, near_prefix), slots)
        for near, place in enumerate((group, neighbour_group())):
            span_scores = products(queries, span_part(span_refs, near, 0))
            scores.append(jnp.where(place < source, span_scores, -jnp.inf))
            values.append(span_part(span_refs, near, 1))
        pack_state(out_ref, *settle(base, scores, values, largest(scores)))

    by_counts(counts_ref, own_prefix.shape[1] // BLOCK, body)


def visit(by, counts, batch, prefixes, spans):
    count, size = batch.shape
    keys = prefixes[0].shape[1] + len(spans) * spans[0].shape[2]
    return pl.pallas_call(
        functools.partial(visit_kernel, math.log2(math.e) / math.sqrt(size), by),
        out_shape=jax.ShapeDtypeStruct((count + tail_rows(count)[1], size), BF16),
        in_specs=[IN_SMEM] + [IN_VMEM] * (3 + len(spans)),
        out_specs=IN_VMEM,
        compiler_params=params(16 * count * keys),
        cost_estimate=cost(1000),
        name="visit",
    )(counts, batch, *prefixes, *spans)


def store_state(out_ref, top, total, blend):
    size = blend.shape[1]
    out_ref[:, :size] = blend
    out_ref[:, size:] = columns_of([top, total], blend.shape[0])


def load_state(ref, rows):
    size = ref.shape[1] - BLOCK
    return ref[rows, size : size + 1], ref[rows, size + 1 : size + 2], ref[rows, :size]


def attend_kernel(base, counts_ref, *refs):
    batch_refs, (own_prefix, near_prefix, out_ref) = refs[:-3], refs[-3:]

    def body(slots):
        queries = jnp.concatenate([ref[...] for ref in batch_refs], axis=0)
        scores, values = prefix_part(queries, counts_ref, (own_prefix, near_prefix), slots)
        store_state(out_ref, *settle(base, scores, values, largest(scores)))

    by_counts(counts_ref, own_prefix.shape[1] // BLOCK, body)


def attend(counts, batches, prefixes):
    size = batches[0].shape[1]
    count = sum(batch.shape[0] for batch in batches)
    return pl.pallas_call(
        functools.partial(attend_kernel, math.log2(math.e) / math.sqrt(size)),
        out_shape=jax.ShapeDtypeStruct((count, size + BLOCK), F32),
        in_specs=[IN_SMEM] + [IN_VMEM] * (2 + len(batches)),
        out_specs=IN_VMEM,
        compiler_params=params(16 * count * prefixes[0].shape[1]),
        cost_estimate=cost(5),
        name="attend",
    )(counts, *batches, *prefixes)


def finish_visit_kernel(base, by, batch_ref, state_ref, *refs):
    span_refs, out_ref = refs[:-1], refs[-1]
    groups = lax.axis_size("ctx")
    group = lax.axis_index("ctx")
    source = lax.rem(group + groups - by, groups)
    queries = batch_ref[...]
    scores, values = [], []
    for near, place in enumerate((group, neighbour_group())):
        span_scores = products(queries, span_part(span_refs, near, 0))
        scores.append(jnp.where(place < source, span_scores, -jnp.inf))
        values.append(span_part(span_refs, near, 1))
    state = load_state(state_ref, slice(None))
    top = jnp.maximum(state[0], largest(scores))
    pack_state(out_ref, *settle(base, scores, values, top, state))


def finish_visit(by, batch, state, spans):
    count, size = batch.shape
    return pl.pallas_call(
        functools.partial(finish_visit_kernel, math.log2(math.e) / math.sqrt(size), by),
        out_shape=jax.ShapeDtypeStruct((count + tail_rows(count)[1], size), BF16),
        in_specs=[IN_VMEM] * (2 + len(spans)),
        out_specs=IN_VMEM,
        compiler_params=params(64 * count * size),
        cost_estimate=cost(1000),
        name="finish_visit",
    )(batch, state, *spans)


def part_state(ref, count):
    tiles, _ = tail_rows(count)
    lines = ref[count:, :].astype(F32)
    lines = jnp.concatenate([lines[8 * i : 8 * i + 8] for i in range(tiles)], axis=1)
    filler = jnp.zeros((BLOCK - 8, tiles * BLOCK), F32)
    tile = jnp.transpose(jnp.concatenate([lines, filler], axis=0))[:count]
    top = tile[:, 0:1] + tile[:, 1:2] + tile[:, 2:3]
    total = tile[:, 3:4] + tile[:, 4:5] + tile[:, 5:6]
    return top, total, ref[:count, :].astype(F32)


def merged(base, parts):
    top = functools.reduce(jnp.maximum, [part[0] for part in parts])
    total, blend = 0.0, 0.0
    for part_top, part_sum, part_blend in parts:
        shrink = jnp.exp2((part_top - top) * base)
        total = total + part_sum * shrink
        blend = blend + part_blend * shrink
    return (blend / total).astype(BF16)


def merge_one_kernel(base, spans, width, one_ref, two_ref, own_ref, own_weight, other_weight, *refs):
    span_refs = refs[:spans]
    state_ref, own_columns, other_columns, sems = refs[spans:]
    core = lax.rem(lax.axis_index("head"), CORES)
    copies = column_copies(width, core, own_weight, own_columns, sems.at[0])
    copies += column_copies(width, core, other_weight, other_columns, sems.at[1])
    total_count = own_ref.shape[0]
    own_rows = span_refs[0].shape[2]
    tokens = spans * own_rows
    group = lax.axis_index("ctx")

    def with_spans(queries, rows):
        query = token_ids((total_count, 1), 0, own_rows, total_count // tokens)
        visible = (token_ids((1, tokens), 1, own_rows, 1) <= query)[rows]
        state = load_state(own_ref, rows)
        scores = [
            jnp.where(visible, products(queries, span_part(span_refs, 0, 0)), -jnp.inf),
            jnp.where(
                neighbour_group() < group, products(queries, span_part(span_refs, 1, 0)), -jnp.inf
            ),
        ]
        values = [span_part(span_refs, near, 1) for near in range(2)]
        top = jnp.maximum(state[0], largest(scores))
        return settle(base, scores, values, top, state)

    @pl.when(group >= 0)
    def _():
        queries = jnp.concatenate([one_ref[...], two_ref[...]], axis=0)
        store_state(state_ref, *with_spans(queries, slice(None)))

    for copy in copies:
        copy.wait()


def merge_one(batches, spans, own, weights, width):
    one, two = batches
    size = one.shape[1]
    shape = (weights[0].shape[0], weights[0].shape[1] // CORES)
    return pl.pallas_call(
        functools.partial(
            merge_one_kernel, math.log2(math.e) / math.sqrt(size), len(spans), width
        ),
        out_shape=(
            jax.ShapeDtypeStruct(own.shape, F32),
            pltpu.VMEM(shape, BF16),
            pltpu.VMEM(shape, BF16),
        ),
        in_specs=[IN_VMEM] * 3 + [IN_HBM, ANYWHERE] + [IN_VMEM] * len(spans),
        out_specs=(IN_VMEM,) * 3,
        scratch_shapes=[pltpu.SemaphoreType.DMA((CORES, COLUMN_PIECES, shape[1] // width))],
        compiler_params=params(64 * own.shape[0] * size + 4 * math.prod(shape)),
        cost_estimate=cost(200),
        name="merge_one",
    )(one, two, own, in_hbm(weights[0]), weights[1], *spans)


def merge_mid_kernel(base, state_ref, *refs):
    part_refs, out_ref = refs[:-1], refs[-1]
    count = out_ref.shape[0]
    parts = [load_state(state_ref, slice(0, count))]
    parts += [part_state(ref, count) for ref in part_refs]
    out_ref[...] = merged(base, parts)


def merge_mid(count, state, parts):
    size = parts[0].shape[1]
    return pl.pallas_call(
        functools.partial(merge_mid_kernel, math.log2(math.e) / math.sqrt(size)),
        out_shape=jax.ShapeDtypeStruct((count, size), BF16),
        in_specs=[IN_VMEM] * (1 + len(parts)),
        out_specs=IN_VMEM,
        compiler_params=params(16 * state.shape[0] * size),
        cost_estimate=cost(100),
        name="merge_mid",
    )(state, *parts)


def merge_two_kernel(base, own_rows, rest_ref, one_ref, *refs):
    part_refs, out_ref = refs[:-1], refs[-1]
    tokens = out_ref.shape[0]
    count, size = one_ref.shape
    heads = count // own_rows
    rest_count = rest_ref.shape[0] - count
    parts = [load_state(rest_ref, slice(count, rest_ref.shape[0]))]
    parts += [part_state(ref, rest_count) for ref in part_refs]
    rest = merged(base, parts)
    for piece in range(tokens // own_rows):
        target = pl.ds(pl.multiple_of(piece_row(piece) * own_rows, 16), own_rows)
        for head in range(heads):
            if piece == 0:
                part = one_ref[head * own_rows : (head + 1) * own_rows, :]
            else:
                at = ((piece - 1) * heads + head) * own_rows
                part = rest[at : at + own_rows]
            out_ref[target, head * size : (head + 1) * size] = part


def merge_two(own_rows, tokens, rest, one, parts):
    count, size = one.shape
    return pl.pallas_call(
        functools.partial(merge_two_kernel, math.log2(math.e) / math.sqrt(size), own_rows),
        out_shape=jax.ShapeDtypeStruct((tokens, count // own_rows * size), BF16),
        in_specs=[IN_VMEM] * (2 + len(parts)),
        out_specs=IN_VMEM,
        compiler_params=params(16 * rest.shape[0] * size),
        cost_estimate=cost(100),
        name="merge_two",
    )(rest, one, *parts)


def block_columns(offsets, width):
    core = lax.rem(lax.axis_index("head"), CORES)
    chip_by, row_by = (
        jnp.where(core == 0, first, second) for first, second in zip(*offsets, strict=True)
    )
    rows = lax.axis_size("row")
    chips = lax.axis_size("head") // CORES
    chip = lax.rem(lax.axis_index("head") // CORES + chip_by, chips)
    row = lax.rem(lax.axis_index("row") + row_by, rows)
    return pl.ds(pl.multiple_of((chip * rows + row) * width, width), width)


def own_share_kernel(offsets, attended_ref, weight, out_ref):
    for place, offset in enumerate(offsets):
        columns = block_columns(offset, out_ref.shape[2])
        out_ref[place] = jnp.dot(
            attended_ref[...], weight[:, columns], preferred_element_type=F32
        )


def own_share(offsets, attended, weight, width):
    shape = (len(offsets), attended.shape[0], width)
    return pl.pallas_call(
        functools.partial(own_share_kernel, offsets),
        out_shape=jax.ShapeDtypeStruct(shape, F32),
        in_specs=[IN_VMEM] * 2,
        out_specs=IN_VMEM,
        compiler_params=params(2 * weight.size + 8 * math.prod(shape)),
        cost_estimate=cost(50),
        name="own_share",
    )(attended, in_vmem(weight))


def out_block_kernel(place, offset, attended_ref, weight, share_ref, out_ref):
    columns = block_columns(offset, out_ref.shape[1])
    block = jnp.dot(attended_ref[...], weight[:, columns], preferred_element_type=F32)
    out_ref[...] = (share_ref[place] + block).astype(out_ref.dtype)


def out_block(place, offset, attended, weight, share, dtype):
    shape = share.shape[1:]
    return pl.pallas_call(
        functools.partial(out_block_kernel, place, offset),
        out_shape=jax.ShapeDtypeStruct(shape, dtype),
        in_specs=[IN_VMEM] * 3,
        out_specs=IN_VMEM,
        compiler_params=params(2 * weight.size + 4 * share.size + 8 * math.prod(shape)),
        cost_estimate=cost(10),
        name="out_block",
    )(attended, in_vmem(weight), share)


def add_block_kernel(total_ref, block_ref, out_ref):
    out_ref[...] = (total_ref[...] + block_ref[...].astype(F32)).astype(out_ref.dtype)


def add_block(total, block, dtype):
    return pl.pallas_call(
        add_block_kernel,
        out_shape=jax.ShapeDtypeStruct(total.shape, dtype),
        in_specs=[IN_VMEM] * 2,
        out_specs=IN_VMEM,
        compiler_params=params(12 * total.size),
        cost_estimate=cost(10),
        name="add_block",
    )(total, block)


def shifted(value, axis, by):
    peers = lax.axis_size(axis)
    return lax.ppermute(value, axis, [(i, (i + by) % peers) for i in range(peers)])


def swapped(value, axis):
    return lax.ppermute(value, axis, [(i, i ^ 1) for i in range(lax.axis_size(axis))])


def local(
    hidden,
    norm_gain,
    q_weight,
    q_bias,
    key_weight,
    key_bias,
    value_weight,
    value_bias,
    o_weight,
    cached_key_rows,
    cached_value_rows,
    keep_blocks,
    kept_counts,
    span_start,
):
    groups = lax.axis_size("ctx")
    rows = lax.axis_size("row")
    chips = lax.axis_size("head") // CORES
    core = lax.axis_index("head") % CORES
    own_rows, width = hidden.shape
    tokens = own_rows * rows
    head_size = key_weight.shape[1]
    block_width = o_weight.shape[1] // (lax.axis_size("head") * rows)
    half = width // CORES

    normed, own_half, own_prefix = first(
        keep_blocks, hidden, norm_gain.reshape(-1, 128), cached_key_rows, cached_value_rows
    )
    near = [shifted(own_half, "row", by) for by in range(1, rows)]
    near = near[0] if rows == 2 else jnp.concatenate(near)
    near_prefix = swapped(own_prefix, "ctx")

    steps = jnp.arange(head_size // 2, dtype=F32)
    frequency = 1000000.0 ** (-2.0 * steps / head_size)
    positions = (
        span_start[0] + lax.axis_index("ctx") * tokens + jnp.arange(tokens, dtype=jnp.int32)
    )
    angles = positions.astype(F32)[:, None] * frequency[None, :]
    cosine, sine = jnp.cos(angles), jnp.sin(angles)
    turns = jnp.stack(
        [jnp.concatenate([cosine, cosine], axis=1), jnp.concatenate([-sine, sine], axis=1)]
    )
    heads = q_weight.shape[1] // head_size
    biases = [bias.reshape(-1, head_size) for bias in (q_bias, key_bias, value_bias)]

    one, span_rows, weights, biases = project_own(
        normed, (q_weight, key_weight, value_weight), biases, turns
    )
    distances = [2 * step for step in range(1, groups // 2)]
    visitors_one = [shifted(one, "ctx", by) for by in distances]
    near_rows = swapped(span_rows, "ctx")
    near, one, span_rows = lax.optimization_barrier((near, one, span_rows))
    far = swapped(near, "head")
    near, o_weight = lax.optimization_barrier((near, o_weight))
    other_weight = swapped(o_weight, "head")
    part = project_near(near, weights, q_weight.shape[1])
    two = project_far(own_rows, far, weights, part, biases, turns)
    visitors_two = [shifted(two, "ctx", by) for by in distances]
    near_rows, two = lax.optimization_barrier((near_rows, two))
    pack = pack_rows(span_rows, near_rows)
    spans = [pack, *(shifted(pack, "row", by) for by in range(1, rows))]

    prefixes = (own_prefix, near_prefix)
    own_state = attend(kept_counts, (one, two), prefixes)
    visitors_one, own_state = lax.optimization_barrier((visitors_one, own_state))
    states = [attend(kept_counts, (visitor,), prefixes) for visitor in visitors_one]
    back_one = [
        finish_visit(by, visitor, state, spans)
        for by, visitor, state in zip(distances, visitors_one, states, strict=True)
    ]
    parts_one = [
        shifted(back, "ctx", -by) for by, back in zip(distances, back_one, strict=True)
    ]
    visitors_two, back_one = lax.optimization_barrier((visitors_two, back_one))
    back_two = [
        visit(by, kept_counts, visitor, prefixes, spans)
        for by, visitor in zip(distances, visitors_two, strict=True)
    ]
    parts_two = [
        shifted(back, "ctx", -by) for by, back in zip(distances, back_two, strict=True)
    ]
    o_weight, other_weight, back_two = lax.optimization_barrier((o_weight, other_weight, back_two))
    state, own_columns, other_columns = merge_one(
        (one, two), spans, own_state, (o_weight, other_weight), rows * block_width
    )
    parts_one, state = lax.optimization_barrier((parts_one, state))
    attended_one = merge_mid(one.shape[0], state, parts_one)
    parts_two, attended_one = lax.optimization_barrier((parts_two, attended_one))
    attended = merge_two(own_rows, tokens, state, attended_one, parts_two)

    other_attended = swapped(attended, "head")
    offsets = [(a, b) for a in range(chips) for b in range(rows)]
    offsets = sorted(offsets[1:], key=lambda offset: (offset[0] != 0) + (offset[1] != 0))
    swapped_offsets = list(offsets)
    for place in range(0, len(offsets) - 1, 2):
        swapped_offsets[place : place + 2] = offsets[place + 1], offsets[place]
    pairs_of_offsets = [*zip(offsets, swapped_offsets, strict=True), ((0, 0), (0, 0))]
    share = own_share(pairs_of_offsets, attended, own_columns, block_width)
    arrived = []
    for place, by_core in enumerate(pairs_of_offsets):
        stays = place == len(offsets)
        block = out_block(
            place, by_core, other_attended, other_columns, share, F32 if stays else BF16
        )
        other_attended, block = lax.optimization_barrier((other_attended, block))
        if stays:
            total = block
            break
        pairs = []
        for c, (chip_by, row_by) in enumerate(by_core):
            for a in range(chips):
                for b in range(rows):
                    target = ((a + chip_by) % chips * CORES + c) * rows + (b + row_by) % rows
                    pairs.append(((a * CORES + c) * rows + b, target))
        arrived.append(lax.ppermute(block, ("head", "row"), pairs))
    for block in arrived[:-1]:
        total = add_block(total, block, F32)
    return add_block(total, arrived[-1], BF16)


def solution(mesh):
    in_specs = (
        P(("ctx", "row"), None),
        P(),
        P(None, ("head", "row")),
        P(("head", "row")),
        P(None, "head"),
        P("head"),
        P(None, "head"),
        P("head"),
        P(("head", "row"), None),
        P("ctx", "head"),
        P("ctx", "head"),
        P("ctx", None),
        P(),
        P(),
    )
    out_specs = P("ctx", ("head", "row"))
    return jax.shard_map(local, mesh=mesh, in_specs=in_specs, out_specs=out_specs, check_vma=False)
```
